512 devices in a mesh: node: 64 (over z, y_hi, core), local: 8 (over y_lo, x).
Axes of the slice: x: 4, y: 8 (y_hi: 4, y_lo: 2; y = y_hi * 2 + y_lo), z: 8, core: 2. Of those that a mesh axis runs over, the one named last changes fastest.
Arguments:
- tokens: bfloat16 [1536, 4096], P('node', 'local'), may hold values from -6 to 6
- cotangent: bfloat16 [1536, 4096], P('node', 'local'), may hold values from -0.75 to 0.75
- gate_weight: bfloat16 [14336, 4096], P('node', 'local'), may hold values from -0.09375 to 0.09375
- up_weight: bfloat16 [14336, 4096], P('node', 'local'), may hold values from -0.09375 to 0.09375
- down_weight: bfloat16 [14336, 4096], P('node', 'local'), may hold values from -0.046875 to 0.046875
- gate_moment: bfloat16 [14336, 4096], P('node', 'local'), may hold values from -6 to 6
- gate_square: bfloat16 [14336, 4096], P('node', 'local'), may hold values from 0.099609375 to 4
- up_moment: bfloat16 [14336, 4096], P('node', 'local'), may hold values from -6 to 6
- up_square: bfloat16 [14336, 4096], P('node', 'local'), may hold values from 0.099609375 to 4
- down_moment: bfloat16 [14336, 4096], P('node', 'local'), may hold values from -6 to 6
- down_square: bfloat16 [14336, 4096], P('node', 'local'), may hold values from 0.099609375 to 4
Outputs:
- input_grad: bfloat16 [1536, 4096], P('node', 'local')
- moment_gate: bfloat16 [14336, 4096], P('node', 'local')
- square_gate: bfloat16 [14336, 4096], P('node', 'local')
- update_gate: bfloat16 [14336, 4096], P('node', 'local')
- moment_up: bfloat16 [14336, 4096], P('node', 'local')
- square_up: bfloat16 [14336, 4096], P('node', 'local')
- update_up: bfloat16 [14336, 4096], P('node', 'local')
- moment_down: bfloat16 [14336, 4096], P('node', 'local')
- square_down: bfloat16 [14336, 4096], P('node', 'local')
- update_down: bfloat16 [14336, 4096], P('node', 'local')
The draws below stay inside these ranges and needn't reach their ends.
All inputs are finite; a program needn't handle non-finite values.
Results may differ from the reference program's by a relative error of at most 0.0049.
Values may be sent and summed in bfloat16 or wider, within the bound.
A program may use at most 64 MiB of HBM per device.

```python
import math
import jax
import jax.numpy as jnp

D = 4096
FF = 14336
ADAM_STEP = 20
TOKENS = 1536


def steps_of(rng, shape, cuts, least, largest):
    loudness = 1.0
    for axis_at, blocks in cuts:
        heights = jax.random.uniform(jax.random.fold_in(jax.random.fold_in(rng, 6), axis_at), (blocks,), jnp.float32, least / len(cuts), largest / len(cuts))
        loudness = loudness * jnp.repeat(jnp.exp(heights), shape[axis_at] // blocks).reshape((-1,) + (1,) * (len(shape) - 1 - axis_at))
    return loudness


def noise(key, extent, deviation, limit, cuts=(), held_as=jnp.bfloat16):
    values = jax.random.normal(key, extent, jnp.float32) * deviation
    if len(cuts) > 0:
        values = steps_of(key, extent, cuts, -0.22, 0.18) * values
    return jnp.clip(values, min=-limit, max=limit).astype(held_as)


def setup_inputs(seed: int = 0) -> dict:
    key_of = jax.random.split(jax.random.key(seed), 12)
    return {
        "tokens": noise(key_of[0], (TOKENS, D), 1.0, 6.0, ((0, 64), (1, 8))),
        "cotangent": noise(key_of[1], (TOKENS, D), 0.125, 0.75, ((0, 64), (1, 8))),
        "gate_weight": noise(key_of[2], (FF, D), D ** -0.5, 0.09375, ((0, 64), (1, 8))),
        "up_weight": noise(key_of[3], (FF, D), D ** -0.5, 0.09375, ((0, 64), (1, 8))),
        "down_weight": noise(key_of[4], (FF, D), FF ** -0.5, 0.046875, ((0, 64), (1, 8))),
        "gate_moment": noise(key_of[5], (FF, D), 1.0, 6.0, ((0, 64), (1, 8))),
        "gate_square": jnp.clip(jnp.exp(math.log(4.0) - 3.6927934 * jax.random.uniform(key_of[6], (FF, D), jnp.float32) ** steps_of(key_of[6], (FF, D), ((0, 64), (1, 8)), -0.2, 0.2)), 0.099609375, 4.0).astype(jnp.bfloat16),
        "up_moment": noise(key_of[7], (FF, D), 1.0, 6.0, ((0, 64), (1, 8))),
        "up_square": jnp.clip(jnp.exp(math.log(4.0) - 3.6927934 * jax.random.uniform(key_of[8], (FF, D), jnp.float32) ** steps_of(key_of[8], (FF, D), ((0, 64), (1, 8)), -0.2, 0.2)), 0.099609375, 4.0).astype(jnp.bfloat16),
        "down_moment": noise(key_of[9], (FF, D), 1.0, 6.0, ((0, 64), (1, 8))),
        "down_square": jnp.clip(jnp.exp(math.log(4.0) - 3.6927934 * jax.random.uniform(key_of[10], (FF, D), jnp.float32) ** steps_of(key_of[10], (FF, D), ((0, 64), (1, 8)), -0.2, 0.2)), 0.099609375, 4.0).astype(jnp.bfloat16),
    }


beta_one = 0.9
beta_two = 0.95
epsilon = 1e-08

def activate(gate, up, back):
    sigma = jax.nn.sigmoid(gate)
    acted = gate * sigma
    hidden = (acted * up).astype(jnp.bfloat16)
    gate_grad = (back * up * sigma * (1.0 + gate * (1.0 - sigma))).astype(jnp.bfloat16)
    up_grad = (back * acted).astype(jnp.bfloat16)
    return (hidden, gate_grad, up_grad)

def adam_step(gradient, moment, square):
    moment_new = beta_one * moment.astype(jnp.float32) + (1.0 - beta_one) * gradient
    square_new = beta_two * square.astype(jnp.float32) + (1.0 - beta_two) * gradient * gradient
    scaled = moment_new / (1.0 - beta_one ** ADAM_STEP)
    spread = jnp.sqrt(square_new / (1.0 - beta_two ** ADAM_STEP)) + epsilon
    return (moment_new.astype(jnp.bfloat16), square_new.astype(jnp.bfloat16), (scaled / spread).astype(jnp.bfloat16))

def reference(tokens, cotangent, gate_weight, up_weight, down_weight, gate_moment, gate_square, up_moment, up_square, down_moment, down_square):
    gate = jnp.dot(tokens, gate_weight.T, preferred_element_type=jnp.float32)
    up = jnp.dot(tokens, up_weight.T, preferred_element_type=jnp.float32)
    back = jnp.dot(cotangent, down_weight.T, preferred_element_type=jnp.float32)
    hidden, gate_grad, up_grad = activate(gate, up, back)
    input_grad = jnp.dot(gate_grad, gate_weight, preferred_element_type=jnp.float32)
    input_grad = input_grad + jnp.dot(up_grad, up_weight, preferred_element_type=jnp.float32)
    input_grad = input_grad.astype(jnp.bfloat16)
    grad_gate = jnp.dot(gate_grad.T, tokens, preferred_element_type=jnp.float32)
    grad_up = jnp.dot(up_grad.T, tokens, preferred_element_type=jnp.float32)
    grad_down = jnp.dot(hidden.T, cotangent, preferred_element_type=jnp.float32)
    moment_gate, square_gate, update_gate = adam_step(grad_gate, gate_moment, gate_square)
    moment_up, square_up, update_up = adam_step(grad_up, up_moment, up_square)
    moment_down, square_down, update_down = adam_step(grad_down, down_moment, down_square)
    return (input_grad, moment_gate, square_gate, update_gate, moment_up, square_up, update_up, moment_down, square_down, update_down)
```

```python
import functools

import jax
import jax.numpy as jnp
from jax import lax
from jax.experimental import pallas as pl
from jax.experimental.pallas import tpu as pltpu
from jax.sharding import PartitionSpec as P

ADAM_STEP = 20


beta_one = 0.9
beta_two = 0.95
epsilon = 1e-08

NZ, NYH, NC, NYL, NX = 8, 4, 2, 2, 4
MESH = pl.DeviceIdType.MESH
CHUNKS = ((0, 7), (1, 6), (2, 5), (3, 4))
PAD = 256


def adam_step(gradient, moment, square):
    moment_new = beta_one * moment.astype(jnp.float32) + (1.0 - beta_one) * gradient
    square_new = beta_two * square.astype(jnp.float32) + (1.0 - beta_two) * gradient * gradient
    scaled = moment_new / (1.0 - beta_one**ADAM_STEP)
    spread = jnp.sqrt(square_new / (1.0 - beta_two**ADAM_STEP)) + epsilon
    return (
        moment_new.astype(jnp.bfloat16),
        square_new.astype(jnp.bfloat16),
        (scaled / spread).astype(jnp.bfloat16),
    )


def nt(a, b):
    return lax.dot_general(a, b, (((1,), (1,)), ((), ())), preferred_element_type=jnp.float32)


def nn(a, b):
    return lax.dot_general(a, b, (((1,), (0,)), ((), ())), preferred_element_type=jnp.float32)


def tn(a, b):
    return lax.dot_general(a, b, (((0,), (0,)), ((), ())), preferred_element_type=jnp.float32)


def kernel(
    tok, cot, gw, uw, dw, ig, g_out,
    own_s, r_a, zb, wb, p_f, p_b, r_b, a_b, i_own, i_out, i_in, y_b, r_y, z_f, r_z, g_s, g_r,
    s_w, t_w, l_w, s_a, t_a, s_z, t_z, s_c, t_c, s_b, t_b, s_h, t_h, s_d, t_d, s_y, t_y, s_o, t_o, s_g, t_g,
):
    rows, feat = tok.shape
    units = gw.shape[0]
    block = NYH * rows
    chunk = 2 * block
    slice_ = chunk // NX
    node, local = lax.axis_index("node"), lax.axis_index("local")
    z, yh, c = node // (NYH * NC), (node // NC) % NYH, node % NC
    yl, x = local // NX, local % NX

    def at(dz=0, dyh=0, core=c, low=yl, dx=0):
        return (
            (((z + dz) % NZ) * NYH + (yh + dyh) % NYH) * NC + core,
            low * NX + (x + dx) % NX,
        )

    sibling, pair = at(core=1 - c), at(low=1 - yl)
    swapped = c != yl

    pending = []

    def send(src, dst, out, arrive, to):
        copy = pltpu.make_async_remote_copy(
            src_ref=src, dst_ref=dst, send_sem=out, recv_sem=arrive, device_id=to, device_id_type=MESH
        )
        copy.start()
        pending.append(copy)
        return copy

    own_w = []
    for p, ref in enumerate((gw, uw, dw)):
        copy = pltpu.make_async_copy(ref, wb.at[yl, p, pl.ds(0, units)], l_w.at[p])
        copy.start()
        own_w.append(copy)

    barrier = pltpu.get_barrier_semaphore()
    partners = [sibling, pair]
    partners += [at(dz=k) for k in range(1, NZ)]
    partners += [at(dx=k) for k in range(1, NX)]
    partners += [at(dyh=k, core=yl, low=c) for k in range(1, NYH)]
    for to in partners:
        pl.semaphore_signal(barrier, inc=1, device_id=to, device_id_type=MESH)

    @pl.when(swapped)
    def _():
        pl.semaphore_signal(barrier, inc=1, device_id=at(core=yl, low=c), device_id_type=MESH)

    own_s[...] = jnp.concatenate(
        [tok[...].astype(jnp.float32), cot[...].astype(jnp.float32)], axis=0
    ).astype(jnp.bfloat16)
    for h in range(2):
        for p in range(3):
            wb[h, p, units:PAD, :] = jnp.zeros((PAD - units, feat), jnp.bfloat16)
    pl.semaphore_wait(barrier, len(partners) + (c + yl) % 2)

    a_copies = []
    for k in range(1, NYH):
        a_copies.append(send(own_s, r_a.at[yh], s_a.at[k], t_a.at[k], at(dyh=k, core=yl, low=c)))
    here = pltpu.make_async_remote_copy(
        src_ref=own_s, dst_ref=r_a.at[yh], send_sem=s_a.at[0], recv_sem=t_a.at[0],
        device_id=at(core=yl, low=c), device_id_type=MESH,
    )

    @pl.when(swapped)
    def _():
        here.start()

    @pl.when(jnp.logical_not(swapped))
    def _():
        r_a[yh] = own_s[...]

    w_copies = []
    for p, ref in enumerate((gw, uw, dw)):
        w_copies.append(send(ref, wb.at[yl, p, pl.ds(0, units)], s_w.at[p], t_w.at[p], pair))

    for copy in a_copies:
        copy.wait_recv()

    @pl.when(swapped)
    def _():
        here.wait()

    for kind in range(2):
        zb[c, 0, kind] = jnp.concatenate(
            [r_a[j].astype(jnp.float32)[kind * rows : (kind + 1) * rows] for j in range(NYH)], axis=0
        ).astype(jnp.bfloat16)

    to_sibling = {}

    def share(slot, kind):
        to_sibling[slot, kind] = send(
            zb.at[c, slot, kind], zb.at[c, slot, kind], s_c.at[slot, kind], t_c.at[slot, kind], sibling
        )

    ring = {}

    def forward(step):
        for kind in range(2):
            if step < NZ // 2 or kind == 0:
                ring[0, step, kind] = send(
                    zb.at[c, (NZ - step + 1) % NZ, kind], zb.at[c, NZ - step, kind],
                    s_z.at[0, step - 1, kind], t_z.at[0, step - 1, kind], at(dz=1),
                )
            if step < NZ // 2 or kind == 1:
                ring[1, step, kind] = send(
                    zb.at[c, step - 1, kind], zb.at[c, step, kind],
                    s_z.at[1, step - 1, kind], t_z.at[1, step - 1, kind], at(dz=NZ - 1),
                )

    def ring_step(step):
        last = step == NZ // 2
        for kind in range(2):
            for way in range(2):
                if (way, step, kind) in ring:
                    ring[way, step, kind].wait_recv()
            if not last:
                nxt = step + 1
                if nxt < NZ // 2 or kind == 0:
                    ring[0, nxt, kind] = send(
                        zb.at[c, NZ - step, kind], zb.at[c, NZ - nxt, kind],
                        s_z.at[0, step, kind], t_z.at[0, step, kind], at(dz=1),
                    )
                if nxt < NZ // 2 or kind == 1:
                    ring[1, nxt, kind] = send(
                        zb.at[c, step, kind], zb.at[c, nxt, kind],
                        s_z.at[1, step, kind], t_z.at[1, step, kind], at(dz=NZ - 1),
                    )
                share(NZ - step, kind)
                share(step, kind)
            else:
                share(step, kind)

    def wide(h, k, kind):
        first, second = CHUNKS[k]
        return jnp.concatenate([zb[h, first, kind], zb[h, second, kind]], axis=0)

    b_copies, c_copies, d_copies, y_copies, o_copies = {}, {}, {}, {}, {}

    def products(k):
        for slot in CHUNKS[k]:
            for kind in range(2):
                to_sibling[slot, kind].wait_recv()
        gate_up = jnp.zeros((chunk, 2 * PAD), jnp.float32)
        back = jnp.zeros((chunk, PAD), jnp.float32)
        for h in range(2):
            gate_up += nt(wide(h, k, 0), wb[h, 0:2].reshape(2 * PAD, feat))
            back += nt(wide(h, k, 1), wb[h, 2])
        p_f[k, :, 0 : 2 * PAD] = gate_up
        p_f[k, :, 2 * PAD :] = back
        p_b[k, :, 0 : 2 * PAD] = gate_up.astype(jnp.bfloat16)
        p_b[k, :, 2 * PAD :] = back.astype(jnp.bfloat16)
        for d in range(1, NX):
            theirs = pl.multiple_of(((x + d) % NX) * slice_, slice_)
            b_copies[k, d] = send(
                p_b.at[k, pl.ds(theirs, slice_)], r_b.at[k, d - 1], s_b.at[k, d - 1], t_b.at[k, d - 1], at(dx=d)
            )

    def activate(k):
        for d in range(1, NX):
            b_copies[k, d].wait_recv()
        mine = pl.ds(pl.multiple_of(x * slice_, slice_), slice_)
        total = p_f[k, mine]
        for d in range(1, NX):
            total += r_b[k, d - 1].astype(jnp.float32)
        gate, up, back = total[:, :PAD], total[:, PAD : 2 * PAD], total[:, 2 * PAD :]
        sigma = jax.nn.sigmoid(gate)
        acted = gate * sigma
        a_b[k, mine, 0:PAD] = (back * up * sigma * (1.0 + gate * (1.0 - sigma))).astype(jnp.bfloat16)
        a_b[k, mine, PAD : 2 * PAD] = (back * acted).astype(jnp.bfloat16)
        a_b[k, mine, 2 * PAD :] = (acted * up).astype(jnp.bfloat16)
        for d in range(1, NX):
            c_copies[k, d] = send(
                a_b.at[k, mine], a_b.at[k, mine], s_h.at[k, d - 1], t_h.at[k, d - 1], at(dx=d)
            )

    def input_part(k):
        for d in range(1, NX):
            c_copies[k, d].wait_recv()
        grads = a_b[k, :, 0 : 2 * PAD]
        i_out[k] = nn(grads, wb[1 - c, 0:2].reshape(2 * PAD, feat))
        d_copies[k] = send(i_out.at[k], i_in.at[k], s_d.at[k], t_d.at[k], sibling)
        i_own[k] = nn(grads, wb[c, 0:2].reshape(2 * PAD, feat))

    def over_y(k):
        d_copies[k].wait_recv()
        total = i_own[k] + i_in[k]
        for j in range(NYH):
            y_b[k, j] = jnp.concatenate(
                [total[j * rows : (j + 1) * rows], total[block + j * rows : block + (j + 1) * rows]], axis=0
            ).astype(jnp.bfloat16)
        for d in range(1, NYH):
            y_copies[k, d] = send(
                y_b.at[k, (yh + d) % NYH], r_y.at[k, d], s_y.at[k, d], t_y.at[k, d], at(dyh=d, core=yl, low=c)
            )
        straight = pltpu.make_async_remote_copy(
            src_ref=y_b.at[k, yh], dst_ref=r_y.at[k, 0], send_sem=s_y.at[k, 0], recv_sem=t_y.at[k, 0],
            device_id=at(core=yl, low=c), device_id_type=MESH,
        )
        y_copies[k, 0] = straight

        @pl.when(swapped)
        def _():
            straight.start()

        @pl.when(jnp.logical_not(swapped))
        def _():
            r_y[k, 0] = y_b[k, yh]

    def over_z(k):
        for d in range(1, NYH):
            y_copies[k, d].wait_recv()

        @pl.when(swapped)
        def _():
            y_copies[k, 0].wait()

        total = r_y[k, 0].astype(jnp.float32)
        for d in range(1, NYH):
            total += r_y[k, d].astype(jnp.float32)
        for n, slot in enumerate(CHUNKS[k]):
            z_f[slot] = total[n * rows : (n + 1) * rows]
            if slot != 0:
                o_copies[slot] = send(
                    z_f.at[slot], r_z.at[slot - 1], s_o.at[slot - 1], t_o.at[slot - 1], at(dz=slot)
                )

    g_copies = []

    def tokens_of(h, kind):
        return jnp.concatenate([zb[h, slot, kind] for pair_ in CHUNKS for slot in pair_], axis=0)

    acts = (0, 1, 2)
    kinds = (0, 0, 1)

    def weight_parts_out():
        for p in acts:
            grads = a_b[:, :, p * PAD : (p + 1) * PAD].reshape(len(CHUNKS) * chunk, PAD)
            part = tn(grads, tokens_of(1 - yl, kinds[p]))
            g_s[p] = part[:units].astype(jnp.bfloat16)
            g_copies.append(send(g_s.at[p], g_r.at[p], s_g.at[p], t_g.at[p], pair))

    def weight_parts_own():
        for p in acts:
            grads = a_b[:, :, p * PAD : (p + 1) * PAD].reshape(len(CHUNKS) * chunk, PAD)
            g_out[p] = tn(grads, tokens_of(yl, kinds[p]))[:units]

    forward(1)
    for kind in range(2):
        share(0, kind)
    for copy in own_w:
        copy.wait()
    ring_step(1)
    for copy in w_copies:
        copy.wait_recv()
    products(0)
    ring_step(2)
    products(1)
    activate(0)
    ring_step(3)
    products(2)
    activate(1)
    input_part(0)
    ring_step(4)
    products(3)
    activate(2)
    input_part(1)
    over_y(0)
    activate(3)
    input_part(2)
    over_y(1)
    over_z(0)
    input_part(3)
    weight_parts_out()
    over_y(2)
    over_y(3)
    over_z(1)
    weight_parts_own()
    over_z(2)
    over_z(3)
    for slot in range(1, NZ):
        o_copies[slot].wait_recv()
    total = z_f[0]
    for slot in range(1, NZ):
        total += r_z[slot - 1]
    ig[...] = total.astype(jnp.bfloat16)
    for p in acts:
        g_copies[p].wait_recv()
        g_out[p] += g_r[p].astype(jnp.float32)
    for copy in pending:
        copy.wait_send()


def per_device(
    tokens,
    cotangent,
    gate_weight,
    up_weight,
    down_weight,
    gate_moment,
    gate_square,
    up_moment,
    up_square,
    down_moment,
    down_square,
):
    rows, feat = tokens.shape
    units = gate_weight.shape[0]
    block = NYH * rows
    chunk = 2 * block
    part = chunk // NX
    n = len(CHUNKS)
    bf, f32 = jnp.bfloat16, jnp.float32
    dma = pltpu.SemaphoreType.DMA
    vmem = pl.BlockSpec(memory_space=pltpu.VMEM)
    anywhere = pl.BlockSpec(memory_space=pl.ANY)
    sems = [(3,), (3,), (3,)]
    sems += [(NYH,)] * 2
    sems += [(2, NZ // 2, 2)] * 2
    sems += [(NZ, 2)] * 2
    sems += [(n, NX - 1)] * 4
    sems += [(n,)] * 2
    sems += [(n, NYH)] * 2
    sems += [(NZ - 1,)] * 2
    sems += [(3,)] * 2
    input_grad, grads = pl.pallas_call(
        kernel,
        name="ffn_step",
        out_shape=(
            jax.ShapeDtypeStruct((rows, feat), bf),
            jax.ShapeDtypeStruct((3, units, feat), f32),
        ),
        in_specs=[vmem, vmem, anywhere, anywhere, anywhere],
        out_specs=(vmem, vmem),
        scratch_shapes=[
            pltpu.VMEM((2 * rows, feat), bf),
            pltpu.VMEM((NYH, 2 * rows, feat), bf),
            pltpu.VMEM((2, NZ, 2, block, feat), bf),
            pltpu.VMEM((2, 3, PAD, feat), bf),
            pltpu.VMEM((n, chunk, 3 * PAD), f32),
            pltpu.VMEM((n, chunk, 3 * PAD), bf),
            pltpu.VMEM((n, NX - 1, part, 3 * PAD), bf),
            pltpu.VMEM((n, chunk, 3 * PAD), bf),
            pltpu.VMEM((n, chunk, feat), f32),
            pltpu.VMEM((n, chunk, feat), f32),
            pltpu.VMEM((n, chunk, feat), f32),
            pltpu.VMEM((n, NYH, 2 * rows, feat), bf),
            pltpu.VMEM((n, NYH, 2 * rows, feat), bf),
            pltpu.VMEM((NZ, rows, feat), f32),
            pltpu.VMEM((NZ - 1, rows, feat), f32),
            pltpu.VMEM((3, units, feat), bf),
            pltpu.VMEM((3, units, feat), bf),
        ]
        + [dma(shape) for shape in sems],
        compiler_params=pltpu.CompilerParams(
            collective_id=0, has_side_effects=True, vmem_limit_bytes=48 * 2**20
        ),
    )(tokens, cotangent, gate_weight, up_weight, down_weight)
    moment_gate, square_gate, update_gate = adam_step(grads[0], gate_moment, gate_square)
    moment_up, square_up, update_up = adam_step(grads[1], up_moment, up_square)
    moment_down, square_down, update_down = adam_step(grads[2], down_moment, down_square)
    return (
        input_grad,
        moment_gate,
        square_gate,
        update_gate,
        moment_up,
        square_up,
        update_up,
        moment_down,
        square_down,
        update_down,
    )


def solution(mesh):
    spec = P("node", "local")
    return jax.shard_map(
        per_device,
        mesh=mesh,
        in_specs=(spec,) * 11,
        out_specs=(spec,) * 10,
        check_vma=False,
    )
```

```python
import functools

import jax
import jax.numpy as jnp
from jax import lax
from jax.experimental import pallas as pl
from jax.experimental.pallas import tpu as pltpu
from jax.sharding import PartitionSpec as P

ADAM_STEP = 20


beta_one = 0.9
beta_two = 0.95
epsilon = 1e-08

NZ, NYH, NC, NYL, NX = 8, 4, 2, 2, 4
MESH = pl.DeviceIdType.MESH
CHUNKS = ((0, 7), (1, 6), (2, 5), (3, 4))
UB = 128
STRIP = 16


def adam_step(gradient, moment, square):
    moment_new = beta_one * moment.astype(jnp.float32) + (1.0 - beta_one) * gradient
    square_new = beta_two * square.astype(jnp.float32) + (1.0 - beta_two) * gradient * gradient
    scaled = moment_new * (1.0 / (1.0 - beta_one**ADAM_STEP))
    spread = jnp.sqrt(square_new * (1.0 / (1.0 - beta_two**ADAM_STEP))) + epsilon
    return (
        moment_new.astype(jnp.bfloat16),
        square_new.astype(jnp.bfloat16),
        (scaled / spread).astype(jnp.bfloat16),
    )


def nt(a, b):
    return lax.dot_general(a, b, (((1,), (1,)), ((), ())), preferred_element_type=jnp.float32)


def nn(a, b):
    return lax.dot_general(a, b, (((1,), (0,)), ((), ())), preferred_element_type=jnp.float32)


def tn(a, b):
    return lax.dot_general(a, b, (((0,), (0,)), ((), ())), preferred_element_type=jnp.float32)


def kernel(
    tok, cot, gw, uw, dw, gm, gs, um, us, dm, ds, ig, steps,
    raw, own_s, r_a, zb, wb, p_f, p_b, r_b, a_b, i_own, i_out, i_in, z_b, r_z, y_f, r_y, g_o, g_s, g_r, mv, o_v,
    l_t, l_m, l_o, l_w, s_w, t_w, s_a, t_a, s_z, t_z, s_c, t_c, s_b, t_b, s_h, t_h, s_d, t_d, s_o, t_o, s_y, t_y, s_g, t_g,
):
    rows, feat = tok.shape
    units = gw.shape[0]
    block = NYH * rows
    chunk = 2 * block
    slice_ = chunk // NX
    n_chunks = len(CHUNKS)
    cuts = ((0, UB), (UB, units - UB))
    node, local = lax.axis_index("node"), lax.axis_index("local")
    z, yh, c = node // (NYH * NC), (node // NC) % NYH, node % NC
    yl, x = local // NX, local % NX

    def at(dz=0, dyh=0, core=c, low=yl, dx=0):
        return (
            (((z + dz) % NZ) * NYH + (yh + dyh) % NYH) * NC + core,
            low * NX + (x + dx) % NX,
        )

    sibling, pair = at(core=1 - c), at(low=1 - yl)
    swapped = c != yl

    def send(src, dst, out, arrive, to):
        copy = pltpu.make_async_remote_copy(
            src_ref=src, dst_ref=dst, send_sem=out, recv_sem=arrive, device_id=to, device_id_type=MESH
        )
        copy.start()
        return copy

    def bytes_of(ref, sem):
        pltpu.make_async_copy(ref, ref, sem).wait()

    for kind, ref in enumerate((tok, cot)):
        pltpu.make_async_copy(ref, raw.at[kind], l_t).start()

    barrier = pltpu.get_barrier_semaphore()
    partners = [sibling, pair] + [at(dz=k) for k in range(1, NZ)]
    partners += [at(dx=k) for k in range(1, NX)]
    partners += [at(dyh=k, core=yl, low=c) for k in range(1, NYH)]
    for to in partners:
        pl.semaphore_signal(barrier, inc=1, device_id=to, device_id_type=MESH)

    @pl.when(swapped)
    def _():
        pl.semaphore_signal(barrier, inc=1, device_id=at(core=yl, low=c), device_id_type=MESH)

    for f, (first, count) in enumerate(cuts):
        for p, ref in enumerate((gw, uw, dw)):
            pltpu.make_async_copy(
                ref.at[pl.ds(first, count)], wb.at[yl, f, p, pl.ds(0, count)], l_w
            ).start()
    for p, refs in enumerate(((gm, gs), (um, us), (dm, ds))):
        for j, ref in enumerate(refs):
            pltpu.make_async_copy(ref, mv.at[p, j], l_m).start()
    for h in range(2):
        for p in range(3):
            wb[h, 1, p, units - UB :, :] = jnp.zeros((2 * UB - units, feat), jnp.bfloat16)
    bytes_of(raw, l_t)
    own_s[...] = jnp.concatenate(
        [raw[kind].astype(jnp.float32) for kind in range(2)], axis=0
    ).astype(jnp.bfloat16)
    pl.semaphore_wait(barrier, len(partners) + (c + yl) % 2)

    for k in range(1, NYH):
        send(own_s, r_a.at[yh], s_a.at[1], t_a.at[1], at(dyh=k, core=yl, low=c))
    here = pltpu.make_async_remote_copy(
        src_ref=own_s, dst_ref=r_a.at[yh], send_sem=s_a.at[0], recv_sem=t_a.at[0],
        device_id=at(core=yl, low=c), device_id_type=MESH,
    )

    @pl.when(swapped)
    def _():
        here.start()

    @pl.when(jnp.logical_not(swapped))
    def _():
        r_a[yh] = own_s[...]

    def weights_out(f):
        first, count = cuts[f]
        for p, ref in enumerate((gw, uw, dw)):
            send(ref.at[pl.ds(first, count)], wb.at[yl, f, p, pl.ds(0, count)], s_w, t_w.at[f], pair)

    def weights_in(f):
        bytes_of(wb.at[1 - yl, f, :, pl.ds(0, cuts[f][1])], t_w.at[f])

    ring = {}
    chunk_of = {slot: k for k, slots in enumerate(CHUNKS) for slot in slots}

    def share(slot, kind):
        send(zb.at[c, slot, kind], zb.at[c, slot, kind], s_c, t_c.at[chunk_of[slot]], sibling)

    def forward(step, kind, way):
        if step > NZ // 2 or (step == NZ // 2 and kind != way):
            return
        src, dst = ((NZ - step + 1) % NZ, NZ - step) if way == 0 else (step - 1, step)
        ring[way, step, kind] = send(
            zb.at[c, src, kind], zb.at[c, dst, kind],
            s_z, t_z.at[way, step - 1, kind], at(dz=1 if way == 0 else NZ - 1),
        )

    def ring_step(step):
        for kind in range(2):
            for way in range(2):
                if (way, step, kind) in ring:
                    ring[way, step, kind].wait_recv()
                    forward(step + 1, kind, way)
                    share(NZ - step if way == 0 else step, kind)

    def tokens_in():
        bytes_of(r_a.at[pl.ds(0, NYH - 1)], t_a.at[1])

        @pl.when(swapped)
        def _():
            here.wait()

        for kind in range(2):
            zb[c, 0, kind] = jnp.concatenate(
                [r_a[j].astype(jnp.float32)[kind * rows : (kind + 1) * rows] for j in range(NYH)], axis=0
            ).astype(jnp.bfloat16)
            for way in range(2):
                forward(1, kind, way)
        for kind in range(2):
            share(0, kind)

    def wide(h, k, kind):
        first, second = CHUNKS[k]
        return jnp.concatenate([zb[h, first, kind], zb[h, second, kind]], axis=0)

    shared = set()

    def siblings_in(k):
        if k not in shared:
            shared.add(k)
            bytes_of(zb.at[1 - c, pl.ds(0, 2)], t_c.at[k])

    d_copies = {}

    def products(f, k):
        siblings_in(k)
        gate_up = nt(wide(0, k, 0), wb[0, f, 0:2].reshape(2 * UB, feat))
        gate_up += nt(wide(1, k, 0), wb[1, f, 0:2].reshape(2 * UB, feat))
        back = nt(wide(0, k, 1), wb[0, f, 2])
        back += nt(wide(1, k, 1), wb[1, f, 2])
        p_f[f, k, :, 0 : 2 * UB] = gate_up
        p_f[f, k, :, 2 * UB :] = back
        p_b[f, k, :, 0 : 2 * UB] = gate_up.astype(jnp.bfloat16)
        p_b[f, k, :, 2 * UB :] = back.astype(jnp.bfloat16)
        for d in range(1, NX):
            theirs = pl.multiple_of(((x + d) % NX) * slice_, slice_)
            send(p_b.at[f, k, pl.ds(theirs, slice_)], r_b.at[f, k, d - 1], s_b, t_b.at[f, k], at(dx=d))

    def activate(f, k):
        bytes_of(r_b.at[f, k], t_b.at[f, k])
        mine = pl.ds(pl.multiple_of(x * slice_, slice_), slice_)
        total = p_f[f, k, mine]
        for d in range(1, NX):
            total += r_b[f, k, d - 1].astype(jnp.float32)
        gate, up, back = total[:, :UB], total[:, UB : 2 * UB], total[:, 2 * UB :]
        sigma = jax.nn.sigmoid(gate)
        acted = gate * sigma
        a_b[f, k, mine, 0:UB] = (back * up * sigma * (1.0 + gate * (1.0 - sigma))).astype(jnp.bfloat16)
        a_b[f, k, mine, UB : 2 * UB] = (back * acted).astype(jnp.bfloat16)
        a_b[f, k, mine, 2 * UB :] = (acted * up).astype(jnp.bfloat16)
        for d in range(1, NX):
            send(a_b.at[f, k, mine], a_b.at[f, k, mine], s_h, t_h.at[f, k], at(dx=d))

    def gathered(f, k):
        bytes_of(r_b.at[f, k], t_h.at[f, k])

    def input_part(k):
        def half(h):
            total = nn(a_b[0, k, :, 0 : 2 * UB], wb[h, 0, 0:2].reshape(2 * UB, feat))
            return total + nn(a_b[1, k, :, 0 : 2 * UB], wb[h, 1, 0:2].reshape(2 * UB, feat))

        i_out[k] = half(1 - c)
        d_copies[k] = send(i_out.at[k], i_in.at[k], s_d, t_d.at[k], sibling)
        i_own[k] = half(c)

    def over_z(k):
        d_copies[k].wait_recv()
        for n, slot in enumerate(CHUNKS[k]):
            part = slice(n * block, (n + 1) * block)
            total = i_own[k, part] + i_in[k, part]
            if slot == 0:
                y_f[...] = total
            else:
                z_b[slot - 1] = total.astype(jnp.bfloat16)
                send(z_b.at[slot - 1], r_z.at[slot - 1], s_o, t_o, at(dz=slot))

    def over_y():
        bytes_of(r_z, t_o)
        total = y_f[...]
        for slot in range(1, NZ):
            total += r_z[slot - 1].astype(jnp.float32)
        y_f[...] = total

        def part(j):
            return pl.ds(pl.multiple_of(j * rows, 8), rows)

        for d in range(1, NYH):
            send(y_f.at[part((yh + d) % NYH)], r_y.at[d], s_y.at[1], t_y.at[1], at(dyh=d, core=yl, low=c))
        straight = pltpu.make_async_remote_copy(
            src_ref=y_f.at[part(yh)], dst_ref=r_y.at[0], send_sem=s_y.at[0], recv_sem=t_y.at[0],
            device_id=at(core=yl, low=c), device_id_type=MESH,
        )

        @pl.when(swapped)
        def _():
            straight.start()

        @pl.when(jnp.logical_not(swapped))
        def _():
            r_y[0] = y_f[part(yh)]

        return straight

    def input_out(straight):
        bytes_of(r_y.at[pl.ds(1, NYH - 1)], t_y.at[1])

        @pl.when(swapped)
        def _():
            straight.wait()

        total = r_y[0]
        for d in range(1, NYH):
            total += r_y[d]
        ig[...] = total.astype(jnp.bfloat16)

    def tokens_of(h, kind):
        return jnp.concatenate([zb[h, slot, kind] for pair_ in CHUNKS for slot in pair_], axis=0)

    def weight_parts(f, h):
        grads = a_b[f].reshape(n_chunks * chunk, 3 * UB)
        both = tn(grads[:, : 2 * UB], tokens_of(h, 0))
        return both[:UB], both[UB:], tn(grads[:, 2 * UB :], tokens_of(h, 1))

    def weights_grad_pair(f):
        for p, part in enumerate(weight_parts(f, 1 - yl)):
            g_s[f, p] = part.astype(jnp.bfloat16)

    def weights_grad_out(f):
        count = cuts[f][1]
        for p in range(3):
            send(g_s.at[f, p, pl.ds(0, count)], g_r.at[f, p, pl.ds(0, count)], s_g, t_g.at[f], pair)

    def weights_grad_own(f):
        for p, part in enumerate(weight_parts(f, yl)):
            g_o[f, p] = part

    def adam(f):
        first, count = cuts[f]
        bytes_of(g_r.at[f, :, pl.ds(0, count)], t_g.at[f])
        for p in range(3):

            @pl.loop(0, count // STRIP)
            def _(i):
                here_ = pl.ds(pl.multiple_of(i * STRIP, STRIP), STRIP)
                there = pl.ds(pl.multiple_of(first + i * STRIP, STRIP), STRIP)
                gradient = g_o[f, p, here_] + g_r[f, p, here_].astype(jnp.float32)
                for j, value in enumerate(adam_step(gradient, mv[p, 0, there], mv[p, 1, there])):
                    o_v[3 * p + j, there] = value

            for j in range(3):
                part = pl.ds(first, count)
                pltpu.make_async_copy(o_v.at[3 * p + j, part], steps.at[3 * p + j, part], l_o).start()

    def sent_early():
        bytes_of(r_a.at[pl.ds(0, NYH - 1)], s_a.at[1])
        bytes_of(mv.at[:, 0], s_w)
        bytes_of(zb.at[0, pl.ds(0, NZ - 1)], s_z)
        bytes_of(zb.at[0], s_c)
        bytes_of(r_b, s_b)
        bytes_of(r_b, s_h)
        bytes_of(i_out, s_d)

    weights_out(0)
    tokens_in()
    weights_out(1)
    bytes_of(mv.at[:, 0], l_w)
    ring_step(1)
    weights_in(0)
    products(0, 0)
    ring_step(2)
    products(0, 1)
    activate(0, 0)
    weights_in(1)
    products(1, 0)
    products(1, 1)
    ring_step(3)
    products(0, 2)
    products(1, 2)
    activate(0, 1)
    activate(1, 0)
    ring_step(4)
    products(0, 3)
    products(1, 3)
    activate(1, 1)
    activate(0, 2)
    activate(1, 2)
    gathered(0, 0)
    gathered(1, 0)
    input_part(0)
    activate(0, 3)
    over_z(0)
    activate(1, 3)
    gathered(0, 1)
    gathered(1, 1)
    input_part(1)
    over_z(1)
    gathered(0, 2)
    gathered(1, 2)
    input_part(2)
    gathered(0, 3)
    weights_grad_pair(0)
    weights_grad_out(0)
    over_z(2)
    gathered(1, 3)
    input_part(3)
    weights_grad_pair(1)
    over_z(3)
    weights_grad_out(1)
    weights_grad_own(0)
    weights_grad_own(1)
    bytes_of(mv, l_m)
    sent_early()
    adam(0)
    straight = over_y()
    adam(1)
    bytes_of(z_b, s_o)
    bytes_of(mv.at[:, 0], s_g)
    bytes_of(o_v, l_o)
    input_out(straight)
    bytes_of(r_y.at[pl.ds(1, NYH - 1)], s_y.at[1])


def settle(ig, steps, *outs_and_sems):
    outs, sems = outs_and_sems[:-1], outs_and_sems[-1]
    copies = [pltpu.make_async_copy(ig, outs[0], sems.at[0])]
    for j in range(len(outs) - 1):
        copies.append(pltpu.make_async_copy(steps.at[j], outs[j + 1], sems.at[j + 1]))
    for copy in copies:
        copy.start()
    for copy in copies:
        copy.wait()


def per_device(
    tokens,
    cotangent,
    gate_weight,
    up_weight,
    down_weight,
    gate_moment,
    gate_square,
    up_moment,
    up_square,
    down_moment,
    down_square,
):
    rows, feat = tokens.shape
    units = gate_weight.shape[0]
    block = NYH * rows
    chunk = 2 * block
    part = chunk // NX
    n = len(CHUNKS)
    bf, f32 = jnp.bfloat16, jnp.float32
    dma = pltpu.SemaphoreType.DMA
    vmem = pl.BlockSpec(memory_space=pltpu.VMEM)
    hbm = pl.BlockSpec(memory_space=pltpu.HBM)
    sems = [(), (), (), ()]
    sems += [(), (2,)]
    sems += [(2,), (2,)]
    sems += [(), (2, NZ // 2, 2)]
    sems += [(), (n,)]
    sems += [(), (2, n), (), (2, n)]
    sems += [(), (n,)]
    sems += [(), ()]
    sems += [(2,), (2,)]
    sems += [(), (2,)]
    input_grad, steps = pl.pallas_call(
        kernel,
        name="ffn_step",
        out_shape=(
            jax.ShapeDtypeStruct((rows, feat), bf),
            jax.ShapeDtypeStruct((9, units, feat), bf),
        ),
        in_specs=[hbm] * 11,
        out_specs=(vmem, hbm),
        scratch_shapes=[
            pltpu.VMEM((2, rows, feat), bf),
            pltpu.VMEM((2 * rows, feat), bf),
            pltpu.VMEM((NYH, 2 * rows, feat), bf),
            pltpu.VMEM((2, NZ, 2, block, feat), bf),
            pltpu.VMEM((2, 2, 3, UB, feat), bf),
            pltpu.VMEM((2, n, chunk, 3 * UB), f32),
            pltpu.VMEM((2, n, chunk, 3 * UB), bf),
            pltpu.VMEM((2, n, NX - 1, part, 3 * UB), bf),
            pltpu.VMEM((2, n, chunk, 3 * UB), bf),
            pltpu.VMEM((n, chunk, feat), f32),
            pltpu.VMEM((n, chunk, feat), f32),
            pltpu.VMEM((n, chunk, feat), f32),
            pltpu.VMEM((NZ - 1, block, feat), bf),
            pltpu.VMEM((NZ - 1, block, feat), bf),
            pltpu.VMEM((block, feat), f32),
            pltpu.VMEM((NYH, rows, feat), f32),
            pltpu.VMEM((2, 3, UB, feat), f32),
            pltpu.VMEM((2, 3, UB, feat), bf),
            pltpu.VMEM((2, 3, UB, feat), bf),
            pltpu.VMEM((3, 2, units, feat), bf),
            pltpu.VMEM((9, units, feat), bf),
        ]
        + [dma(shape) if shape else dma for shape in sems],
        compiler_params=pltpu.CompilerParams(
            collective_id=0, has_side_effects=True, vmem_limit_bytes=60 * 2**20
        ),
    )(
        tokens, cotangent, gate_weight, up_weight, down_weight,
        gate_moment, gate_square, up_moment, up_square, down_moment, down_square,
    )
    return tuple(
        pl.pallas_call(
            settle,
            name="settle",
            out_shape=(jax.ShapeDtypeStruct((rows, feat), bf),)
            + (jax.ShapeDtypeStruct((units, feat), bf),) * 9,
            in_specs=[vmem, vmem],
            out_specs=(hbm,) * 10,
            scratch_shapes=[dma((10,))],
        )(input_grad, steps)
    )


def solution(mesh):
    spec = P("node", "local")
    return jax.shard_map(
        per_device,
        mesh=mesh,
        in_specs=(spec,) * 11,
        out_specs=(spec,) * 10,
        check_vma=False,
    )
```

```python
import functools

import jax
import jax.numpy as jnp
from jax import lax
from jax.experimental import pallas as pl
from jax.experimental.pallas import tpu as pltpu
from jax.sharding import PartitionSpec as P

ADAM_STEP = 20


beta_one = 0.9
beta_two = 0.95
epsilon = 1e-08

NZ, NYH, NC, NYL, NX = 8, 4, 2, 2, 4
MESH = pl.DeviceIdType.MESH
CHUNKS = ((1, 7), (2, 6), (3, 5), (0, 4))
FIRST, UB = 96, 128
STRIP = 16


def adam_step(gradient, moment, square):
    moment_new = beta_one * moment.astype(jnp.float32) + (1.0 - beta_one) * gradient
    square_new = beta_two * square.astype(jnp.float32) + (1.0 - beta_two) * gradient * gradient
    scaled = moment_new * (1.0 / (1.0 - beta_one**ADAM_STEP))
    spread = jnp.sqrt(square_new * (1.0 / (1.0 - beta_two**ADAM_STEP))) + epsilon
    return (
        moment_new.astype(jnp.bfloat16),
        square_new.astype(jnp.bfloat16),
        (scaled / spread).astype(jnp.bfloat16),
    )


def nt(a, b):
    return lax.dot_general(a, b, (((1,), (1,)), ((), ())), preferred_element_type=jnp.float32)


def nn(a, b):
    return lax.dot_general(a, b, (((1,), (0,)), ((), ())), preferred_element_type=jnp.float32)


def tn(a, b):
    return lax.dot_general(a, b, (((0,), (0,)), ((), ())), preferred_element_type=jnp.float32)


def kernel(
    tok, cot, gw, uw, dw, gm, gs, um, us, dm, ds, ig, steps,
    raw, own_s, r_a, zb, wb, p_f, p_b, r_b, a_b, i_own, i_out, i_in, z_b, r_z, y_f, y_h, r_y, g_o, g_s, g_r, mv, o_v,
    l_t, l_m, l_o, l_w, s_w, t_w, s_a, t_a, s_z, t_z, s_c, t_c, s_b, t_b, s_h, t_h, s_d, t_d, s_o, t_o, s_y, t_y, s_g, t_g,
):
    rows, feat = tok.shape
    units = gw.shape[0]
    block = NYH * rows
    chunk = 2 * block
    slice_ = chunk // NX
    n_chunks = len(CHUNKS)
    cuts = ((0, FIRST), (FIRST, units - FIRST))
    node, local = lax.axis_index("node"), lax.axis_index("local")
    z, yh, c = node // (NYH * NC), (node // NC) % NYH, node % NC
    yl, x = local // NX, local % NX

    def at(dz=0, dyh=0, core=c, low=yl, dx=0):
        return (
            (((z + dz) % NZ) * NYH + (yh + dyh) % NYH) * NC + core,
            low * NX + (x + dx) % NX,
        )

    sibling, pair = at(core=1 - c), at(low=1 - yl)
    swapped = c != yl

    def send(src, dst, out, arrive, to):
        copy = pltpu.make_async_remote_copy(
            src_ref=src, dst_ref=dst, send_sem=out, recv_sem=arrive, device_id=to, device_id_type=MESH
        )
        copy.start()
        return copy

    def bytes_of(ref, sem):
        pltpu.make_async_copy(ref, ref, sem).wait()

    for kind, ref in enumerate((tok, cot)):
        pltpu.make_async_copy(ref, raw.at[kind], l_t).start()

    barrier = pltpu.get_barrier_semaphore()
    partners = [sibling, pair] + [at(dz=k) for k in range(1, NZ)]
    partners += [at(dx=k) for k in range(1, NX)]
    partners += [at(dyh=k, core=yl, low=c) for k in range(1, NYH)]
    for to in partners:
        pl.semaphore_signal(barrier, inc=1, device_id=to, device_id_type=MESH)

    @pl.when(swapped)
    def _():
        pl.semaphore_signal(barrier, inc=1, device_id=at(core=yl, low=c), device_id_type=MESH)

    bytes_of(raw, l_t)
    own_s[...] = jnp.concatenate(
        [raw[kind].astype(jnp.float32) for kind in range(2)], axis=0
    ).astype(jnp.bfloat16)
    pl.semaphore_wait(barrier, len(partners) + (c + yl) % 2)

    for k in range(1, NYH):
        send(own_s, r_a.at[yh], s_a.at[1], t_a.at[1], at(dyh=k, core=yl, low=c))
    here = pltpu.make_async_remote_copy(
        src_ref=own_s, dst_ref=r_a.at[yh], send_sem=s_a.at[0], recv_sem=t_a.at[0],
        device_id=at(core=yl, low=c), device_id_type=MESH,
    )

    @pl.when(swapped)
    def _():
        here.start()

    @pl.when(jnp.logical_not(swapped))
    def _():
        r_a[yh] = own_s[...]

    def weights_out(f):
        first, count = cuts[f]
        for p, ref in enumerate((gw, uw, dw)):
            send(ref.at[pl.ds(first, count)], wb.at[yl, f, p, pl.ds(0, count)], s_w, t_w.at[f], pair)

    def weights_in(f):
        bytes_of(wb.at[1 - yl, f, :, pl.ds(0, cuts[f][1])], t_w.at[f])

    def own_in():
        for f, (first, count) in enumerate(cuts):
            for p, ref in enumerate((gw, uw, dw)):
                pltpu.make_async_copy(
                    ref.at[pl.ds(first, count)], wb.at[yl, f, p, pl.ds(0, count)], l_w
                ).start()
        for p, refs in enumerate(((gm, gs), (um, us), (dm, ds))):
            for j, ref in enumerate(refs):
                pltpu.make_async_copy(ref, mv.at[p, j], l_m).start()
        for f, (_, count) in enumerate(cuts):
            for h in range(2):
                for p in range(3):
                    if count < UB:
                        wb[h, f, p, count:, :] = jnp.zeros((UB - count, feat), jnp.bfloat16)

    ring = {}
    chunk_of = {slot: k for k, slots in enumerate(CHUNKS) for slot in slots}

    def share(slot, kind):
        send(zb.at[c, slot, kind], zb.at[c, slot, kind], s_c, t_c.at[chunk_of[slot]], sibling)

    def forward(step, kind, way):
        if step > NZ // 2 or (step == NZ // 2 and kind != way):
            return
        src, dst = ((NZ - step + 1) % NZ, NZ - step) if way == 0 else (step - 1, step)
        ring[way, step, kind] = send(
            zb.at[c, src, kind], zb.at[c, dst, kind],
            s_z, t_z.at[way, step - 1, kind], at(dz=1 if way == 0 else NZ - 1),
        )

    def ring_step(step):
        for kind in range(2):
            for way in range(2):
                if (way, step, kind) in ring:
                    ring[way, step, kind].wait_recv()
                    forward(step + 1, kind, way)
                    share(NZ - step if way == 0 else step, kind)

    def tokens_in():
        bytes_of(r_a.at[pl.ds(0, NYH - 1)], t_a.at[1])

        @pl.when(swapped)
        def _():
            here.wait()

        for kind in range(2):
            zb[c, 0, kind] = jnp.concatenate(
                [r_a[j].astype(jnp.float32)[kind * rows : (kind + 1) * rows] for j in range(NYH)], axis=0
            ).astype(jnp.bfloat16)
            for way in range(2):
                forward(1, kind, way)
        for kind in range(2):
            share(0, kind)

    def wide(h, k, kind):
        first, second = CHUNKS[k]
        return jnp.concatenate([zb[h, first, kind], zb[h, second, kind]], axis=0)

    shared = set()

    def siblings_in(k):
        if k not in shared:
            shared.add(k)
            bytes_of(zb.at[1 - c, pl.ds(0, 2)], t_c.at[k])

    d_copies = {}

    def products(f, k):
        siblings_in(k)
        gate_up = nt(wide(0, k, 0), wb[0, f, 0:2].reshape(2 * UB, feat))
        gate_up += nt(wide(1, k, 0), wb[1, f, 0:2].reshape(2 * UB, feat))
        back = nt(wide(0, k, 1), wb[0, f, 2])
        back += nt(wide(1, k, 1), wb[1, f, 2])
        p_f[f, k, :, 0 : 2 * UB] = gate_up
        p_f[f, k, :, 2 * UB :] = back
        p_b[f, k, :, 0 : 2 * UB] = gate_up.astype(jnp.bfloat16)
        p_b[f, k, :, 2 * UB :] = back.astype(jnp.bfloat16)
        for d in range(1, NX):
            theirs = pl.multiple_of(((x + d) % NX) * slice_, slice_)
            send(p_b.at[f, k, pl.ds(theirs, slice_)], r_b.at[f, k, d - 1], s_b, t_b.at[f, k], at(dx=d))

    def activate(f, k):
        bytes_of(r_b.at[f, k], t_b.at[f, k])
        mine = pl.ds(pl.multiple_of(x * slice_, slice_), slice_)
        total = p_f[f, k, mine]
        for d in range(1, NX):
            total += r_b[f, k, d - 1].astype(jnp.float32)
        gate, up, back = total[:, :UB], total[:, UB : 2 * UB], total[:, 2 * UB :]
        sigma = jax.nn.sigmoid(gate)
        acted = gate * sigma
        a_b[f, k, mine, 0:UB] = (back * up * sigma * (1.0 + gate * (1.0 - sigma))).astype(jnp.bfloat16)
        a_b[f, k, mine, UB : 2 * UB] = (back * acted).astype(jnp.bfloat16)
        a_b[f, k, mine, 2 * UB :] = (acted * up).astype(jnp.bfloat16)
        for d in range(1, NX):
            send(a_b.at[f, k, mine], a_b.at[f, k, mine], s_h, t_h.at[f, k], at(dx=d))

    def gathered(f, k):
        bytes_of(r_b.at[f, k], t_h.at[f, k])

    def input_part(k):
        def half(h):
            total = nn(a_b[0, k, :, 0 : 2 * UB], wb[h, 0, 0:2].reshape(2 * UB, feat))
            return total + nn(a_b[1, k, :, 0 : 2 * UB], wb[h, 1, 0:2].reshape(2 * UB, feat))

        i_out[k] = half(1 - c)
        d_copies[k] = send(i_out.at[k], i_in.at[k], s_d, t_d.at[k], sibling)
        i_own[k] = half(c)

    def over_z(k):
        d_copies[k].wait_recv()
        for n, slot in enumerate(CHUNKS[k]):
            part = slice(n * block, (n + 1) * block)
            total = i_own[k, part] + i_in[k, part]
            if slot == 0:
                y_f[...] = total
            else:
                z_b[slot - 1] = total.astype(jnp.bfloat16)
                for h in range(2):
                    there = pl.ds(h * (feat // 2), feat // 2)
                    send(
                        z_b.at[slot - 1, :, there], r_z.at[slot - 1, :, there], s_o, t_o.at[h], at(dz=slot)
                    )

    def over_y(h):
        there = pl.ds(h * (feat // 2), feat // 2)
        bytes_of(r_z.at[:, :, there], t_o.at[h])
        total = y_f[:, there]
        for slot in range(1, NZ):
            total += r_z[slot - 1, :, there].astype(jnp.float32)
        y_h[h] = total

        def part(j):
            return pl.ds(pl.multiple_of(j * rows, 8), rows)

        for d in range(1, NYH):
            send(
                y_h.at[h, part((yh + d) % NYH)], r_y.at[h, d], s_y.at[h, 1], t_y.at[h, 1],
                at(dyh=d, core=yl, low=c),
            )
        straight = pltpu.make_async_remote_copy(
            src_ref=y_h.at[h, part(yh)], dst_ref=r_y.at[h, 0], send_sem=s_y.at[h, 0], recv_sem=t_y.at[h, 0],
            device_id=at(core=yl, low=c), device_id_type=MESH,
        )

        @pl.when(swapped)
        def _():
            straight.start()

        @pl.when(jnp.logical_not(swapped))
        def _():
            r_y[h, 0] = y_h[h, part(yh)]

        return straight

    def input_out(h, straight):
        there = pl.ds(h * (feat // 2), feat // 2)
        bytes_of(r_y.at[h, pl.ds(1, NYH - 1)], t_y.at[h, 1])

        @pl.when(swapped)
        def _():
            straight.wait()

        total = r_y[h, 0]
        for d in range(1, NYH):
            total += r_y[h, d]
        ig[:, there] = total.astype(jnp.bfloat16)
        bytes_of(r_y.at[h, pl.ds(1, NYH - 1)], s_y.at[h, 1])

    def tokens_of(h, kind):
        return jnp.concatenate([zb[h, slot, kind] for pair_ in CHUNKS for slot in pair_], axis=0)

    def weight_parts(f, h):
        grads = a_b[f].reshape(n_chunks * chunk, 3 * UB)
        both = tn(grads[:, : 2 * UB], tokens_of(h, 0))
        return both[:UB], both[UB:], tn(grads[:, 2 * UB :], tokens_of(h, 1))

    def weights_grad_pair(f):
        for p, part in enumerate(weight_parts(f, 1 - yl)):
            g_s[f, p] = part.astype(jnp.bfloat16)

    def weights_grad_out(f):
        count = cuts[f][1]
        for p in range(3):
            send(g_s.at[f, p, pl.ds(0, count)], g_r.at[f, p, pl.ds(0, count)], s_g, t_g.at[f], pair)

    def weights_grad_own(f):
        for p, part in enumerate(weight_parts(f, yl)):
            g_o[f, p] = part

    def adam(f):
        first, count = cuts[f]
        bytes_of(g_r.at[f, :, pl.ds(0, count)], t_g.at[f])
        for p in range(3):

            @pl.loop(0, count // STRIP)
            def _(i):
                here_ = pl.ds(pl.multiple_of(i * STRIP, STRIP), STRIP)
                there = pl.ds(pl.multiple_of(first + i * STRIP, STRIP), STRIP)
                gradient = g_o[f, p, here_] + g_r[f, p, here_].astype(jnp.float32)
                for j, value in enumerate(adam_step(gradient, mv[p, 0, there], mv[p, 1, there])):
                    o_v[3 * p + j, there] = value

            for j in range(3):
                part = pl.ds(first, count)
                pltpu.make_async_copy(o_v.at[3 * p + j, part], steps.at[3 * p + j, part], l_o).start()

    def sent_early():
        bytes_of(r_a.at[pl.ds(0, NYH - 1)], s_a.at[1])
        bytes_of(mv.at[:, 0], s_w)
        bytes_of(zb.at[0, pl.ds(0, NZ - 1)], s_z)
        bytes_of(zb.at[0], s_c)
        bytes_of(r_b, s_b)
        bytes_of(r_b, s_h)
        bytes_of(i_out, s_d)

    weights_out(0)
    own_in()
    tokens_in()
    weights_out(1)
    bytes_of(mv.at[:, 0], l_w)
    ring_step(1)
    weights_in(0)
    products(0, 0)
    ring_step(2)
    products(0, 1)
    activate(0, 0)
    weights_in(1)
    products(1, 0)
    products(1, 1)
    ring_step(3)
    activate(0, 1)
    products(0, 2)
    products(1, 2)
    activate(1, 0)
    ring_step(4)
    activate(1, 1)
    products(0, 3)
    products(1, 3)
    activate(0, 2)
    activate(1, 2)
    gathered(0, 0)
    gathered(1, 0)
    input_part(0)
    activate(0, 3)
    over_z(0)
    activate(1, 3)
    gathered(0, 1)
    gathered(1, 1)
    input_part(1)
    over_z(1)
    gathered(0, 2)
    gathered(1, 2)
    input_part(2)
    gathered(0, 3)
    weights_grad_pair(0)
    weights_grad_out(0)
    over_z(2)
    gathered(1, 3)
    input_part(3)
    weights_grad_pair(1)
    over_z(3)
    weights_grad_out(1)
    weights_grad_own(0)
    weights_grad_own(1)
    bytes_of(mv, l_m)
    sent_early()
    adam(0)
    halves = [over_y(0), over_y(1)]
    adam(1)
    bytes_of(z_b, s_o)
    bytes_of(mv.at[:, 0], s_g)
    bytes_of(o_v, l_o)
    for h in range(2):
        input_out(h, halves[h])


def settle(ig, steps, *rest):
    outs, (ig_v, steps_v, sem_in, sem_out) = rest[:10], rest[10:]
    ways = [(ig, ig_v, outs[0])] + [(steps.at[j], steps_v.at[j], outs[j + 1]) for j in range(9)]
    for n, (src, mid, _) in enumerate(ways):
        pltpu.make_async_copy(src, mid, sem_in.at[n]).start()
    for n, (src, mid, dst) in enumerate(ways):
        pltpu.make_async_copy(src, mid, sem_in.at[n]).wait()
        pltpu.make_async_copy(mid, dst, sem_out.at[n]).start()
    for n, (_, mid, dst) in enumerate(ways):
        pltpu.make_async_copy(mid, dst, sem_out.at[n]).wait()


def per_device(
    tokens,
    cotangent,
    gate_weight,
    up_weight,
    down_weight,
    gate_moment,
    gate_square,
    up_moment,
    up_square,
    down_moment,
    down_square,
):
    rows, feat = tokens.shape
    units = gate_weight.shape[0]
    block = NYH * rows
    chunk = 2 * block
    part = chunk // NX
    n = len(CHUNKS)
    bf, f32 = jnp.bfloat16, jnp.float32
    dma = pltpu.SemaphoreType.DMA
    vmem = pl.BlockSpec(memory_space=pltpu.VMEM)
    hbm = pl.BlockSpec(memory_space=pltpu.HBM)
    sems = [(), (), (), ()]
    sems += [(), (2,)]
    sems += [(2,), (2,)]
    sems += [(), (2, NZ // 2, 2)]
    sems += [(), (n,)]
    sems += [(), (2, n), (), (2, n)]
    sems += [(), (n,)]
    sems += [(), (2,)]
    sems += [(2, 2), (2, 2)]
    sems += [(), (2,)]
    input_grad, steps = pl.pallas_call(
        kernel,
        name="ffn_step",
        out_shape=(
            jax.ShapeDtypeStruct((rows, feat), bf),
            jax.ShapeDtypeStruct((9, units, feat), bf),
        ),
        in_specs=[hbm] * 11,
        out_specs=(vmem, hbm),
        scratch_shapes=[
            pltpu.VMEM((2, rows, feat), bf),
            pltpu.VMEM((2 * rows, feat), bf),
            pltpu.VMEM((NYH, 2 * rows, feat), bf),
            pltpu.VMEM((2, NZ, 2, block, feat), bf),
            pltpu.VMEM((2, 2, 3, UB, feat), bf),
            pltpu.VMEM((2, n, chunk, 3 * UB), f32),
            pltpu.VMEM((2, n, chunk, 3 * UB), bf),
            pltpu.VMEM((2, n, NX - 1, part, 3 * UB), bf),
            pltpu.VMEM((2, n, chunk, 3 * UB), bf),
            pltpu.VMEM((n, chunk, feat), f32),
            pltpu.VMEM((n, chunk, feat), f32),
            pltpu.VMEM((n, chunk, feat), f32),
            pltpu.VMEM((NZ - 1, block, feat), bf),
            pltpu.VMEM((NZ - 1, block, feat), bf),
            pltpu.VMEM((block, feat), f32),
            pltpu.VMEM((2, block, feat // 2), f32),
            pltpu.VMEM((2, NYH, rows, feat // 2), f32),
            pltpu.VMEM((2, 3, UB, feat), f32),
            pltpu.VMEM((2, 3, UB, feat), bf),
            pltpu.VMEM((2, 3, UB, feat), bf),
            pltpu.VMEM((3, 2, units, feat), bf),
            pltpu.VMEM((9, units, feat), bf),
        ]
        + [dma(shape) if shape else dma for shape in sems],
        compiler_params=pltpu.CompilerParams(
            collective_id=0, has_side_effects=True, vmem_limit_bytes=60 * 2**20
        ),
    )(
        tokens, cotangent, gate_weight, up_weight, down_weight,
        gate_moment, gate_square, up_moment, up_square, down_moment, down_square,
    )
    return tuple(
        pl.pallas_call(
            settle,
            name="settle",
            out_shape=(jax.ShapeDtypeStruct((rows, feat), bf),)
            + (jax.ShapeDtypeStruct((units, feat), bf),) * 9,
            in_specs=[hbm, hbm],
            out_specs=(hbm,) * 10,
            scratch_shapes=[
                pltpu.VMEM((rows, feat), bf), pltpu.VMEM((9, units, feat), bf), dma((10,)), dma((10,)),
            ],
        )(input_grad, steps)
    )


def solution(mesh):
    spec = P("node", "local")
    return jax.shard_map(
        per_device,
        mesh=mesh,
        in_specs=(spec,) * 11,
        out_specs=(spec,) * 10,
        check_vma=False,
    )
```
